32 devices in a mesh: lat: 4 (over z), lon: 8 (over y, x, core).
Axes of the slice: x: 2, y: 2, z: 4, core: 2. Of those that a mesh axis runs over, the one named last changes fastest.
Arguments:
- grid_nodes: bfloat16 [32768, 512], P(('lat', 'lon')), may hold values from -6 to 6
- grid_edges: bfloat16 [9216, 512], P(('lat', 'lon')), may hold values from -6 to 6
- grid_sender: int32 [9216], P(('lat', 'lon')), may hold values from 0 to 1023, as said below
- owner_index: int32 [9216], P(('lat', 'lon')), may hold values from -1 to 255, as said below
- mesh_nodes: bfloat16 [8192, 512], P(('lat', 'lon')), may hold values from -6 to 6
- mesh_edges: bfloat16 [16384, 512], P(('lat', 'lon')), may hold values from -6 to 6
- mesh_sender: int32 [16384], P(('lat', 'lon')), may hold values from 0 to 639, as said below
- mesh_receiver: int32 [16384], P(('lat', 'lon')), may hold values from 0 to 255
- w_first: bfloat16 [3, 1536, 512], replicated, may hold values from -0.15625 to 0.15625
- first_bias: float32 [3, 512], replicated, may hold values from -3 to 3
- w_second: bfloat16 [3, 512, 512], replicated, may hold values from -0.25 to 0.25
- norm_gain: float32 [3, 512], replicated, may hold values from 0.25 to 1.75
- mesh_cotangent: bfloat16 [8192, 512], P(('lat', 'lon')), may hold values from -0.0390625 to 0.0390625
- edge_cotangent: bfloat16 [16384, 512], P(('lat', 'lon')), may hold values from -0.0390625 to 0.0390625
Outputs:
- updated_mesh: bfloat16 [8192, 512], P(('lat', 'lon'))
- updated_edges: bfloat16 [16384, 512], P(('lat', 'lon'))
- grad_first: float32 [3, 1536, 512], P(None, 'lat', 'lon')
- grad_second: float32 [3, 512, 512], P(None, 'lat', 'lon')
The draws below stay inside these ranges and needn't reach their ends.
Inputs may be any that keep to these rules, and one draw needn't show every extreme that they name: `grid_sender`: rows of device p, in 9 blocks of 32 by destination offset as in the reference program: the sending grid point (local index) of each slot; entries of unused slots are arbitrary. `owner_index`: rows of device q, in 9 blocks of 32 by source offset as in the reference program, matching the sender's slots: the receiving local mesh node, -1 for an unused slot. The used slots of a block come first. Blocks from beyond the first or last latitude band are unused. Some device receives 32 used slots from every device that sends to it. `mesh_sender`: row of the sender table described in the reference program; no edge refers to a lat neighbour that does not exist.
All inputs are finite; a program needn't handle non-finite values.
Results may differ from the reference program's by a relative error of at most 0.02.
Values may be sent and summed in bfloat16 or wider, within the bound.
A program may use at most 128 MiB of HBM per device.

```python
import jax
import jax.numpy as jnp
from jax import lax

D = 512
FIN = 1536
G_DEV = 1024
M_DEV = 256
CAP = 32
E_M = 512
BORDER = 64
K_COARSE = 4
SLOTS_DEV = 288
GRID = 32768
MESH = 8192
SLOTS = 9216
EDGES = 16384
COARSE = 128
N_LAT = 4
N_LON = 8
DEVICES = 32


def slot_table(key):
    folded = jax.random.fold_in(key, 7101)
    keys = jax.random.split(folded, 5)
    device = jnp.arange(DEVICES, dtype=jnp.int32)
    band_index = device // N_LON
    cycle_index = device % N_LON
    offset = jnp.arange(9, dtype=jnp.int32)
    band_step = offset // 3 - 1
    cycle_step = offset % 3 - 1
    target_band = band_index[:, None] + band_step[None, :]
    exists = (target_band >= 0) & (target_band < N_LAT)
    destination = (target_band + N_LAT) % N_LAT * N_LON + (cycle_index[:, None] + cycle_step[None, :] + N_LON) % N_LON
    pair_counts = jax.random.randint(keys[0], (DEVICES, 9), 0, CAP + 1)
    owner_limit = jax.random.randint(keys[1], (DEVICES,), CAP // 2, CAP + 1)
    pair_counts = jnp.minimum(pair_counts, jnp.take(owner_limit, destination))
    full_owner = jax.random.randint(keys[2], (), 0, DEVICES)
    pair_counts = jnp.where(destination == full_owner, CAP, pair_counts)
    pair_counts = jnp.where(exists, pair_counts, 0)
    is_live = jnp.arange(CAP, dtype=jnp.int32)[None, None, :] < pair_counts[:, :, None]
    sender = jax.random.randint(keys[3], (DEVICES, 9, CAP), 0, G_DEV)
    target = jax.random.randint(keys[4], (DEVICES, 9, CAP), 0, M_DEV)
    return (is_live, sender, target)


def draw_grid_sender(key, part):
    is_live, sender, target = slot_table(key)
    return sender.reshape(-1).astype(jnp.int32)


def draw_owner_index(key, part):
    is_live, sender, target = slot_table(key)
    marked = jnp.where(is_live, target, -1)
    device = jnp.arange(DEVICES, dtype=jnp.int32)
    band_index = device // N_LON
    cycle_index = device % N_LON
    offset = jnp.arange(9, dtype=jnp.int32)
    band_step = offset // 3 - 1
    cycle_step = offset % 3 - 1
    source = (band_index[:, None] + band_step[None, :] + N_LAT) % N_LAT * N_LON + (cycle_index[:, None] + cycle_step[None, :] + N_LON) % N_LON
    flat_index = source * 9 + (8 - offset)[None, :]
    picked = jnp.take(marked.reshape(DEVICES * 9, CAP), flat_index.reshape(-1), axis=0)
    return picked.reshape(-1).astype(jnp.int32)


def draw_mesh_sender(key, part):
    folded = jax.random.fold_in(key, 7202)
    keys = jax.random.split(folded, 6)
    row_count = DEVICES * E_M
    device = jnp.arange(row_count, dtype=jnp.int32) // E_M
    band_index = device // N_LON
    choose_kind = jax.random.randint(keys[0], (row_count,), 0, 100)
    own_pick = jax.random.randint(keys[1], (row_count,), 0, M_DEV)
    border_pick = jax.random.randint(keys[2], (row_count,), 0, BORDER)
    band_side = jax.random.randint(keys[3], (row_count,), 0, 2)
    cycle_side = jax.random.randint(keys[4], (row_count,), 0, 2)
    coarse_pick = jax.random.randint(keys[5], (row_count,), 0, COARSE)
    band_exists = jnp.where(band_side == 0, band_index > 0, band_index < N_LAT - 1)
    band_row = M_DEV + band_side * BORDER + border_pick
    cycle_row = M_DEV + 2 * BORDER + cycle_side * BORDER + border_pick
    coarse_row = M_DEV + 4 * BORDER + coarse_pick
    picked = jnp.where(choose_kind < 55, own_pick, jnp.where(choose_kind < 70, jnp.where(band_exists, band_row, own_pick), jnp.where(choose_kind < 85, cycle_row, coarse_row)))
    return picked.astype(jnp.int32)


def set_ends(result, rng, least, largest):
    shape = result.shape
    spot = [jax.random.randint(jax.random.fold_in(rng, axis), (), 0, shape[axis]) for axis in range(len(shape))]
    result = result.at[tuple(spot)].set(least)
    longest = shape.index(max(shape))
    spot[longest] = (spot[longest] + 1) % shape[longest]
    return result.at[tuple(spot)].set(largest)


def levels(stream_key, dims, shards, least, largest):
    gain, own = 1.0, jax.random.fold_in(stream_key, 6)
    for axis_at, shards_of in shards:
        heights = jnp.exp(jax.random.uniform(jax.random.fold_in(own, axis_at), (shards_of,), jnp.float32, least / len(shards), largest / len(shards)))
        gain = gain * jnp.repeat(heights, dims[axis_at] // shards_of).reshape([-1 if axis == axis_at else 1 for axis in range(len(dims))])
    return gain


def scatter_about(stream_key, dims, scale, limit, pieces=(), kind=jnp.bfloat16):
    entries = scale * jax.random.normal(stream_key, dims, jnp.float32)
    if pieces:
        entries = entries * levels(stream_key, dims, pieces, -0.22, 0.18)
    return jnp.clip(entries, -limit, limit).astype(kind)


def setup_inputs(seed: int = 0) -> dict:
    arg_keys = jax.random.split(jax.random.key(seed), 15)
    return {
        "grid_nodes": scatter_about(arg_keys[0], (GRID, D), 1.0, 6.0, ((0, 32),)),
        "grid_edges": scatter_about(arg_keys[1], (SLOTS, D), 1.0, 6.0, ((0, 32),)),
        "grid_sender": draw_grid_sender(jax.random.fold_in(arg_keys[14], 71), 0),
        "owner_index": draw_owner_index(jax.random.fold_in(arg_keys[14], 71), 0),
        "mesh_nodes": scatter_about(arg_keys[4], (MESH, D), 1.0, 6.0, ((0, 32),)),
        "mesh_edges": scatter_about(arg_keys[5], (EDGES, D), 1.0, 6.0, ((0, 32),)),
        "mesh_sender": draw_mesh_sender(jax.random.fold_in(arg_keys[14], 71), 0),
        "mesh_receiver": set_ends(jax.random.randint(arg_keys[7], (EDGES,), 0, M_DEV), jax.random.fold_in(arg_keys[7], 1), 0, M_DEV - 1).astype(jnp.int32),
        "w_first": scatter_about(arg_keys[8], (3, FIN, D), FIN ** -0.5, 0.15625),
        "first_bias": scatter_about(arg_keys[9], (3, D), 0.5, 3.0, (), jnp.float32),
        "w_second": scatter_about(arg_keys[10], (3, D, D), D ** -0.5, 0.25),
        "norm_gain": jnp.clip(1.0 + 0.15 * jax.random.normal(arg_keys[11], (3, D), jnp.float32), 0.25, 1.75),
        "mesh_cotangent": scatter_about(arg_keys[12], (MESH, D), ((M_DEV + E_M) * DEVICES) ** -0.5, 0.0390625, ((0, 32),)),
        "edge_cotangent": scatter_about(arg_keys[13], (EDGES, D), ((M_DEV + E_M) * DEVICES) ** -0.5, 0.0390625, ((0, 32),)),
    }


EPSILON = 1e-05

def perceptron(inputs, weights, member, pre_shift, out_shift):
    w_first, first_bias, w_second, norm_gain = weights
    preact = jnp.dot(inputs, w_first[member], preferred_element_type=jnp.float32) + first_bias[member] + pre_shift
    hidden = jax.nn.silu(preact).astype(jnp.bfloat16)
    output = jnp.dot(hidden, w_second[member], preferred_element_type=jnp.float32) + out_shift
    centre = lax.optimization_barrier(jnp.mean(output, axis=-1, keepdims=True))
    spread = lax.optimization_barrier(jnp.mean(jnp.square(output - centre), axis=-1, keepdims=True))
    return ((output - centre) * lax.rsqrt(spread + EPSILON) * norm_gain[member], hidden)

def node_sums(receivers, messages, node_count):
    onehot = (receivers[:, None] == jnp.arange(node_count, dtype=jnp.int32)[None, :]).astype(jnp.bfloat16)
    summed = lax.dot_general(onehot, messages, (((0,), (0,)), ((), ())), preferred_element_type=jnp.float32)
    return summed.astype(jnp.bfloat16)

def layer_pass(sender_grid, grid_edge_rows, owner_rows, own_nodes, sender_table, edge_rows, edge_senders, edge_receivers, weights, shifts):
    node_count = own_nodes.shape[0]
    clipped = jnp.maximum(owner_rows, 0)
    grid_input = jnp.concatenate([grid_edge_rows, sender_grid, jnp.take(own_nodes, clipped, axis=0)], axis=1)
    grid_message, grid_hidden = perceptron(grid_input, weights, 0, shifts[0], shifts[1])
    grid_sum = node_sums(owner_rows, grid_message.astype(jnp.bfloat16), node_count)
    edge_input = jnp.concatenate([edge_rows, jnp.take(sender_table, edge_senders, axis=0), jnp.take(own_nodes, edge_receivers, axis=0)], axis=1)
    edge_message, edge_hidden = perceptron(edge_input, weights, 1, shifts[2], shifts[3])
    updated_edges = (edge_rows.astype(jnp.float32) + edge_message).astype(jnp.bfloat16)
    edge_sum = node_sums(edge_receivers, edge_message.astype(jnp.bfloat16), node_count)
    node_input = jnp.concatenate([own_nodes, grid_sum, edge_sum], axis=1)
    node_output, node_hidden = perceptron(node_input, weights, 2, shifts[4], shifts[5])
    updated_mesh = (own_nodes.astype(jnp.float32) + node_output).astype(jnp.bfloat16)
    stored = ((grid_input, grid_hidden), (edge_input, edge_hidden), (node_input, node_hidden))
    return ((updated_mesh, updated_edges), stored)

def forward_backward(sender_grid, grid_edge_rows, owner_rows, own_nodes, sender_table, edge_rows, edge_senders, edge_receivers, weights, mesh_cot, edge_cot):
    feature_width = own_nodes.shape[1]
    row_counts = (owner_rows.shape[0], owner_rows.shape[0], edge_senders.shape[0], edge_senders.shape[0], own_nodes.shape[0], own_nodes.shape[0])
    shifts = tuple((jnp.zeros((row_count, feature_width), jnp.float32) for row_count in row_counts))

    def run_layer(shift_list):
        return layer_pass(sender_grid, grid_edge_rows, owner_rows, own_nodes, sender_table, edge_rows, edge_senders, edge_receivers, weights, shift_list)
    outputs, pullback, stored = jax.vjp(run_layer, shifts, has_aux=True)
    shift_grads = pullback((mesh_cot, edge_cot))[0]
    firsts = []
    seconds = []
    for member in range(3):
        inputs, hidden = stored[member]
        pre_grad = shift_grads[2 * member].astype(jnp.bfloat16)
        out_grad = shift_grads[2 * member + 1].astype(jnp.bfloat16)
        firsts.append(lax.dot_general(inputs, pre_grad, (((0,), (0,)), ((), ())), preferred_element_type=jnp.float32))
        seconds.append(lax.dot_general(hidden, out_grad, (((0,), (0,)), ((), ())), preferred_element_type=jnp.float32))
    return (outputs[0], outputs[1], jnp.stack(firsts), jnp.stack(seconds))

def reference(grid_nodes, grid_edges, grid_sender, owner_index, mesh_nodes, mesh_edges, mesh_sender, mesh_receiver, w_first, first_bias, w_second, norm_gain, mesh_cotangent, edge_cotangent):
    weights = (w_first, first_bias, w_second, norm_gain)
    grid_blocks = grid_nodes.reshape(DEVICES, G_DEV, D)
    edge_blocks = grid_edges.reshape(DEVICES, 9, CAP, D)
    sender_blocks = grid_sender.reshape(DEVICES, 9, CAP)
    owner_blocks = owner_index.reshape(DEVICES, SLOTS_DEV)
    node_blocks = mesh_nodes.reshape(DEVICES, M_DEV, D)
    coarse_rows = node_blocks[:, M_DEV - K_COARSE:].reshape(COARSE, D)
    mesh_edge_blocks = mesh_edges.reshape(DEVICES, E_M, D)
    mesh_sender_blocks = mesh_sender.reshape(DEVICES, E_M)
    mesh_receiver_blocks = mesh_receiver.reshape(DEVICES, E_M)
    mesh_cot_blocks = mesh_cotangent.reshape(DEVICES, M_DEV, D)
    edge_cot_blocks = edge_cotangent.reshape(DEVICES, E_M, D)

    def border_of(device):
        return lax.dynamic_index_in_dim(node_blocks, device, 0, False)[:BORDER]

    def per_device(totals, device):
        band_index = device // N_LON
        cycle_index = device % N_LON
        edge_parts = []
        grid_parts = []
        for offset in range(9):
            band_step = offset // 3 - 1
            cycle_step = offset % 3 - 1
            source = (band_index + band_step + N_LAT) % N_LAT * N_LON + (cycle_index + cycle_step + N_LON) % N_LON
            source_edges = lax.dynamic_index_in_dim(edge_blocks, source, 0, False)[8 - offset]
            source_senders = lax.dynamic_index_in_dim(sender_blocks, source, 0, False)[8 - offset]
            source_grid = lax.dynamic_index_in_dim(grid_blocks, source, 0, False)
            edge_parts.append(source_edges)
            grid_parts.append(jnp.take(source_grid, source_senders, axis=0))
        grid_edge_rows = jnp.concatenate(edge_parts, axis=0)
        sender_grid = jnp.concatenate(grid_parts, axis=0)
        owner_rows = lax.dynamic_index_in_dim(owner_blocks, device, 0, False)
        own_nodes = lax.dynamic_index_in_dim(node_blocks, device, 0, False)
        lower = border_of(jnp.maximum(device - N_LON, 0))
        lower = jnp.where(band_index > 0, lower, jnp.zeros_like(lower))
        upper = border_of(jnp.minimum(device + N_LON, DEVICES - 1))
        upper = jnp.where(band_index < N_LAT - 1, upper, jnp.zeros_like(upper))
        western = border_of(band_index * N_LON + (cycle_index + N_LON - 1) % N_LON)
        eastern = border_of(band_index * N_LON + (cycle_index + 1) % N_LON)
        sender_table = jnp.concatenate([own_nodes, lower, upper, western, eastern, coarse_rows], axis=0)
        updated_mesh, updated_edges, first_term, second_term = forward_backward(sender_grid, grid_edge_rows, owner_rows, own_nodes, sender_table, lax.dynamic_index_in_dim(mesh_edge_blocks, device, 0, False), lax.dynamic_index_in_dim(mesh_sender_blocks, device, 0, False), lax.dynamic_index_in_dim(mesh_receiver_blocks, device, 0, False), weights, lax.dynamic_index_in_dim(mesh_cot_blocks, device, 0, False), lax.dynamic_index_in_dim(edge_cot_blocks, device, 0, False))
        return ((totals[0] + first_term, totals[1] + second_term), (updated_mesh, updated_edges))
    devices = jnp.arange(DEVICES, dtype=jnp.int32)
    initial = (jnp.zeros((3, FIN, D), jnp.float32), jnp.zeros((3, D, D), jnp.float32))
    totals, (mesh_rows, edge_rows) = lax.scan(per_device, initial, devices)
    return (mesh_rows.reshape(MESH, D), edge_rows.reshape(EDGES, D), totals[0], totals[1])
```

```python
import functools

import jax
import jax.numpy as jnp
from jax import lax
from jax.experimental import pallas as pl
from jax.experimental.pallas import tpu as pltpu
from jax.sharding import PartitionSpec as P

BORDER = 64
K_COARSE = 4
EPSILON = 1e-05
LANES = 128
MESH = pl.DeviceIdType.MESH
F32 = jnp.float32
BF16 = jnp.bfloat16


def mm(a, b, ca=1, cb=0):
    return lax.dot_general(a, b, (((ca,), (cb,)), ((), ())), preferred_element_type=F32)


def onehot_t(index, count):
    rows = lax.broadcasted_iota(jnp.int32, (count, index.shape[1]), 0)
    return jnp.where(rows == index, 1.0, 0.0).astype(BF16)


def bits_of(count):
    return count.bit_length() - 1


def plan(nlat, nlon, lanes):
    lat = [("lat", b) for b in range(bits_of(nlat))]
    lon = [("lon", b) for b in range(bits_of(nlon))]
    core, rest = lon[:1], lon[1:]
    orders = [
        core + rest + lat,
        core + rest[1:] + lat + rest[:1],
        core + lat + rest,
    ]
    units = lanes // LANES
    if units >= 4:
        cuts = [0, units // 2, 3 * units // 4, units]
    elif units >= 2:
        cuts = [0, units // 2, units]
    else:
        return [(0, lanes, orders[0])]
    return [
        (cuts[i] * LANES, cuts[i + 1] * LANES, orders[i]) for i in range(len(cuts) - 1)
    ]


def kernel(nlat, nlon, groups, *refs):
    (gn, ge, gs, ow, mn, me_h, ms, mr, wf_h, fb, ws_h, ng, mc_h, ec_h) = refs[:14]
    (um, ue, gout) = refs[14:17]
    ngroups = len(groups)
    g_refs = refs[17 : 17 + ngroups]
    r_refs = refs[17 + ngroups : 17 + 2 * ngroups]
    (
        snd, x0, x1, x2, bord, coarse,
        h0, h1, h2, p0, p1, p2, n0, n1, n2, r0, r1, r2,
        pg0, pg1, pg2, og0, og1, og2,
        wf, ws, mc, ec,
        load_sem, slot_send, slot_recv, side_send, side_recv, row_send, row_recv, col_send, col_recv,
        red_send, red_recv,
    ) = refs[17 + 2 * ngroups :]
    xs, hs, ps, ns, rs = (x0, x1, x2), (h0, h1, h2), (p0, p1, p2), (n0, n1, n2), (r0, r1, r2)
    pgs, ogs = (pg0, pg1, pg2), (og0, og1, og2)
    lat, lon = lax.axis_index("lat"), lax.axis_index("lon")
    nodes, d = mn.shape
    slots = ge.shape[0]
    cap = slots // 9
    edges = ue.shape[0]
    has = {-1: lat > 0, 1: lat < nlat - 1}

    def when(a, action):
        if a == 0:
            action()
        else:
            pl.when(has[a])(action)

    loads = [
        pltpu.make_async_copy(wf_h, wf, load_sem.at[0]),
        pltpu.make_async_copy(ws_h, ws, load_sem.at[1]),
        pltpu.make_async_copy(me_h, x1.at[:, pl.ds(0, d)], load_sem.at[2]),
        pltpu.make_async_copy(mc_h, mc, load_sem.at[3]),
        pltpu.make_async_copy(ec_h, ec, load_sem.at[4]),
    ]
    for copy in loads:
        copy.start()

    barrier = pltpu.get_barrier_semaphore()
    peers = [(lat, lax.rem(lon + s, nlon)) for s in range(1, nlon)]
    peers += [(lax.rem(lat + s, nlat), lon) for s in range(1, nlat)]
    peers += [
        (lax.rem(lat + a, nlat), lax.rem(lon + b, nlon))
        for a in (1, nlat - 1)
        for b in (1, nlon - 1)
    ]
    for peer in peers:
        pl.semaphore_signal(barrier, inc=1, device_id=peer, device_id_type=MESH)

    snd[...] = mm(onehot_t(gs[...], gn.shape[0]), gn[...], 0, 0).astype(BF16)
    per_dev = K_COARSE * d // LANES
    tail = mn[nodes - 16 : nodes, :]
    out_row = lax.broadcasted_iota(jnp.int32, (per_dev, 16), 0)
    in_row = lax.broadcasted_iota(jnp.int32, (per_dev, 16), 1)
    staged = jnp.zeros((per_dev, LANES), F32)
    for q in range(d // LANES):
        pick = (out_row - q * K_COARSE == in_row - (16 - K_COARSE)) & (in_row >= 16 - K_COARSE)
        staged += mm(jnp.where(pick, 1.0, 0.0).astype(BF16), tail[:, q * LANES : (q + 1) * LANES])
    me_row = (lat * nlon + lon) * per_dev
    coarse[pl.ds(pl.multiple_of(me_row, 16), per_dev), :] = staged.astype(BF16)

    @pl.when(lat == 0)
    def _():
        x0[0 : 3 * cap, 0 : 2 * d] = jnp.zeros((3 * cap, 2 * d), BF16)
        bord[0:BORDER, :] = jnp.zeros((BORDER, d), BF16)

    @pl.when(lat == nlat - 1)
    def _():
        x0[6 * cap : 9 * cap, 0 : 2 * d] = jnp.zeros((3 * cap, 2 * d), BF16)
        bord[BORDER : 2 * BORDER, :] = jnp.zeros((BORDER, d), BF16)

    pl.semaphore_wait(barrier, len(peers))

    def slot_copy(o, part):
        a, b = o // 3 - 1, o % 3 - 1
        src = (ge, snd)[part]
        return pltpu.make_async_remote_copy(
            src_ref=src.at[pl.ds(o * cap, cap)],
            dst_ref=x0.at[pl.ds((8 - o) * cap, cap), pl.ds(part * d, d)],
            send_sem=slot_send.at[part, o],
            recv_sem=slot_recv.at[part, 8 - o],
            device_id=(lat + a, lax.rem(lon + b + nlon, nlon)),
            device_id_type=MESH,
        )

    def side_copy(side):
        a, b = ((1, 0), (-1, 0), (0, 1), (0, -1))[side]
        return pltpu.make_async_remote_copy(
            src_ref=mn.at[pl.ds(0, BORDER)],
            dst_ref=bord.at[pl.ds(side * BORDER, BORDER)],
            send_sem=side_send.at[side],
            recv_sem=side_recv.at[side],
            device_id=(lat + a, lax.rem(lon + b + nlon, nlon)),
            device_id_type=MESH,
        )

    side_a = (1, -1, 0, 0)
    remote_slots = [o for o in (0, 2, 6, 8, 1, 7, 3, 5)]
    for o in remote_slots:
        when(o // 3 - 1, lambda o=o: slot_copy(o, 1).start())
    for o in remote_slots:
        when(o // 3 - 1, lambda o=o: slot_copy(o, 0).start())

    def row_copy(s):
        from_row = (lat * nlon + lon) * per_dev
        span = pl.ds(pl.multiple_of(from_row, 16), per_dev)
        return pltpu.make_async_remote_copy(
            src_ref=coarse.at[span], dst_ref=coarse.at[span],
            send_sem=row_send.at[s], recv_sem=row_recv.at[s],
            device_id=(lat, lax.rem(lon + s, nlon)), device_id_type=MESH,
        )

    def row_arrival(s):
        owner = lax.rem(lon - s + nlon, nlon)
        span = pl.ds(pl.multiple_of((lat * nlon + owner) * per_dev, 16), per_dev)
        return pltpu.make_async_remote_copy(
            src_ref=coarse.at[span], dst_ref=coarse.at[span],
            send_sem=row_send.at[s], recv_sem=row_recv.at[s],
            device_id=(lat, owner), device_id_type=MESH,
        )

    def col_copy(s, incoming):
        other = lax.rem(lat - s + nlat, nlat) if incoming else lax.rem(lat + s, nlat)
        owner = other if incoming else lat
        span = pl.ds(pl.multiple_of(owner * nlon * per_dev, 16), nlon * per_dev)
        return pltpu.make_async_remote_copy(
            src_ref=coarse.at[span], dst_ref=coarse.at[span],
            send_sem=col_send.at[s], recv_sem=col_recv.at[s],
            device_id=(other, lon), device_id_type=MESH,
        )

    for s in range(1, nlon):
        row_copy(s).start()
    for side in range(4):
        when(side_a[side], lambda side=side: side_copy(side).start())

    x0[4 * cap : 5 * cap, 0:d] = ge[4 * cap : 5 * cap, :]
    x0[4 * cap : 5 * cap, d : 2 * d] = snd[4 * cap : 5 * cap, :]
    own_t = onehot_t(jnp.maximum(ow[...], 0), nodes)
    x0[:, 2 * d : 3 * d] = mm(own_t, mn[...], 0, 0).astype(BF16)
    recv_t = onehot_t(mr[...], nodes)
    x1[:, 2 * d : 3 * d] = mm(recv_t, mn[...], 0, 0).astype(BF16)
    sender = ms[...]
    n1[...] = mm(onehot_t(sender, nodes), mn[...], 0, 0)

    for s in range(1, nlon):
        row_arrival(s).wait_recv()
    for s in range(1, nlat):
        col_copy(s, False).start()
    for copy in loads[:2]:
        copy.wait()

    def forward(k, lo, size):
        rows = pl.ds(lo, size)
        pre = mm(xs[k][rows, :], wf[k]) + fb[k : k + 1, :]
        ps[k][rows, :] = pre
        hidden = (pre * jax.nn.sigmoid(pre)).astype(BF16)
        hs[k][rows, :] = hidden
        out = mm(hidden, ws[k])
        centred = out - jnp.mean(out, axis=-1, keepdims=True)
        scale = lax.rsqrt(jnp.mean(centred * centred, axis=-1, keepdims=True) + EPSILON)
        normed = centred * scale
        ns[k][rows, :] = normed
        rs[k][rows, :] = scale
        return normed * ng[k : k + 1, :]

    def backward(k, lo, size, dmsg):
        rows = pl.ds(lo, size)
        dn = dmsg * ng[k : k + 1, :]
        normed = ns[k][rows, :]
        dout = rs[k][rows, :] * (
            dn
            - jnp.mean(dn, axis=-1, keepdims=True)
            - normed * jnp.mean(dn * normed, axis=-1, keepdims=True)
        )
        og = dout.astype(BF16)
        ogs[k][rows, :] = og
        dh = mm(og, ws[k], 1, 1).astype(BF16).astype(F32)
        pre = ps[k][rows, :]
        gate = jax.nn.sigmoid(pre)
        pg = (dh * (gate * (1.0 + pre * (1.0 - gate)))).astype(BF16)
        pgs[k][rows, :] = pg
        return pg

    def tiles(count):
        size = 256 if count % 256 == 0 else count
        return [(i * size, size) for i in range(count // size)]

    for j in remote_slots:
        def arrive(j=j):
            slot_copy(8 - j, 0).wait_recv()
            slot_copy(8 - j, 1).wait_recv()
        when(j // 3 - 1, arrive)
    grid_msgs = [forward(0, lo, size).astype(BF16) for lo, size in tiles(slots)]
    grid_t = onehot_t(ow[...], nodes)
    x2[:, 0:d] = mn[...]
    total = 0.0
    for (lo, size), msg in zip(tiles(slots), grid_msgs):
        total += mm(grid_t[:, lo : lo + size], msg)
    x2[:, d : 2 * d] = total.astype(BF16)

    for side in range(4):
        when(-side_a[side], lambda side=side: side_copy(side).wait_recv())
    n1[...] += mm(onehot_t(sender - nodes, 4 * BORDER), bord[...], 0, 0)
    for s in range(1, nlat):
        col_copy(s, True).wait_recv()
    rank = sender - (nodes + 4 * BORDER)
    place = lax.shift_right_logical(rank, 2) * per_dev + (rank & (K_COARSE - 1))
    for q in range(d // LANES):
        target = jnp.where(rank >= 0, place + q * K_COARSE, -1)
        picked = mm(onehot_t(target, coarse.shape[0]), coarse[...], 0, 0)
        span = slice(q * LANES, (q + 1) * LANES)
        x1[:, d + q * LANES : d + (q + 1) * LANES] = (n1[:, span] + picked).astype(BF16)
    loads[2].wait()
    total = 0.0
    for lo, size in tiles(edges):
        msg = forward(1, lo, size)
        ue[lo : lo + size, :] = (x1[lo : lo + size, 0:d].astype(F32) + msg).astype(BF16)
        total += mm(recv_t[:, lo : lo + size], msg.astype(BF16))
    x2[:, 2 * d : 3 * d] = total.astype(BF16)

    loads[3].wait()
    for lo, size in tiles(nodes):
        out = forward(2, lo, size)
        um[lo : lo + size, :] = (mn[lo : lo + size, :].astype(F32) + out).astype(BF16)
        backward(2, lo, size, mc[lo : lo + size, :].astype(F32))

    blocks = nlat * nlon
    steps = bits_of(nlat) + bits_of(nlon)
    first_rows = x0.shape[1] // nlat
    second_rows = d // nlat
    block_cols = d // nlon

    def place_of(order, l, c):
        at = 0
        for axis, bit in order:
            at = at * 2 + (((l if axis == "lat" else c) >> bit) & 1)
        return at

    def make_grads(k):
        width = 256
        for top in range(0, d, width):
            left = mm(pgs[k][:, top : top + width], xs[k][...], 0, 0).astype(BF16)
            right = mm(ogs[k][:, top : top + width], hs[k][...], 0, 0).astype(BF16)
            for g, (lo, hi, order) in enumerate(groups):
                for l in range(nlat):
                    for i in range(width // block_cols):
                        at = place_of(order, l, top // block_cols + i)
                        cols = slice(i * block_cols, (i + 1) * block_cols)
                        end = min(hi, first_rows)
                        if lo < end:
                            g_refs[g][k, at, :, 0 : end - lo] = left[
                                cols, l * first_rows + lo : l * first_rows + end
                            ]
                        start = max(lo, first_rows)
                        if start < hi:
                            g_refs[g][k, at, :, start - lo : hi - lo] = right[
                                cols,
                                l * second_rows + start - first_rows : l * second_rows + hi - first_rows,
                            ]

    def bit_at(order, i):
        axis, bit = order[i]
        return lax.rem((lat if axis == "lat" else lon) // (1 << bit), 2)

    bases = []
    for lo, hi, order in groups:
        base = [0]
        for i in range(steps):
            base.append(base[i] + bit_at(order, i) * (blocks >> (i + 1)))
        bases.append(base)

    def red_copy(k, g, i):
        order = groups[g][2]
        half = blocks >> (i + 1)
        axis, bit = order[i]
        mine = bit_at(order, i)
        shift = (1 - 2 * mine) * (1 << bit)
        peer = (lat + shift, lon) if axis == "lat" else (lat, lon + shift)
        return pltpu.make_async_remote_copy(
            src_ref=g_refs[g].at[k, pl.ds(bases[g][i] + (1 - mine) * half, half)],
            dst_ref=r_refs[g].at[k, pl.ds(blocks - 2 * half, half)],
            send_sem=red_send.at[k, g, i],
            recv_sem=red_recv.at[k, g, i],
            device_id=peer,
            device_id_type=MESH,
        )

    def add(k, g, i, start, count):
        half = blocks >> (i + 1)
        base, landed = bases[g][i + 1], blocks - 2 * half

        def one(j, carry):
            g_refs[g][k, base + start + j] = (
                g_refs[g][k, base + start + j].astype(F32)
                + r_refs[g][k, landed + start + j].astype(F32)
            ).astype(BF16)
            return carry

        lax.fori_loop(0, count, one, 0)

    def progress(k, g, i):
        red_copy(k, g, i).wait_recv()
        if i + 1 < steps:
            quarter = blocks >> (i + 2)
            mine = bit_at(groups[g][2], i + 1)
            add(k, g, i, (1 - mine) * quarter, quarter)
            red_copy(k, g, i + 1).start()
            add(k, g, i, mine * quarter, quarter)
        else:
            lo, hi, _ = groups[g]
            gout[k, :, lo:hi] = (
                g_refs[g][k, bases[g][steps]].astype(F32) + r_refs[g][k, blocks - 2].astype(F32)
            )

    make_grads(2)
    for g in range(ngroups):
        red_copy(2, g, 0).start()

    loads[4].wait()
    sums_cot = mm(pg2[...], wf[2, d : 3 * d, :], 1, 1).astype(BF16)
    for lo, size in tiles(edges):
        back = mm(recv_t[:, lo : lo + size], sums_cot[:, d : 2 * d], 0, 0)
        backward(1, lo, size, ec[lo : lo + size, :].astype(F32) + back)
    make_grads(1)
    for g in range(ngroups):
        red_copy(1, g, 0).start()
    for g in range(ngroups):
        progress(2, g, 0)
    for lo, size in tiles(slots):
        backward(0, lo, size, mm(grid_t[:, lo : lo + size], sums_cot[:, 0:d], 0, 0))
    make_grads(0)
    for g in range(ngroups):
        red_copy(0, g, 0).start()
    at = {2: 1, 1: 0, 0: 0}
    while min(at.values()) < steps:
        for k in (2, 1, 0):
            if at[k] < steps:
                for g in range(ngroups):
                    progress(k, g, at[k])
                at[k] += 1

    for o in remote_slots:
        def gone(o=o):
            slot_copy(o, 0).wait_send()
            slot_copy(o, 1).wait_send()
        when(o // 3 - 1, gone)
    for side in range(4):
        when(side_a[side], lambda side=side: side_copy(side).wait_send())
    for s in range(1, nlon):
        row_copy(s).wait_send()
    for s in range(1, nlat):
        col_copy(s, False).wait_send()
    for k in range(3):
        for g in range(ngroups):
            for i in range(steps):
                red_copy(k, g, i).wait_send()


def shards(
    nlat, nlon,
    grid_nodes, grid_edges, grid_sender, owner_index, mesh_nodes, mesh_edges, mesh_sender,
    mesh_receiver, w_first, first_bias, w_second, norm_gain, mesh_cotangent, edge_cotangent,
):
    d = grid_nodes.shape[1]
    slots, nodes, edges = grid_edges.shape[0], mesh_nodes.shape[0], mesh_edges.shape[0]
    fin = w_first.shape[1]
    blocks = nlat * nlon
    steps = bits_of(nlat) + bits_of(nlon)
    lanes = (fin + d) // nlat
    groups = plan(nlat, nlon, lanes)
    ngroups = len(groups)
    cols = d // nlon
    rows = (slots, edges, nodes)
    vmem = pl.BlockSpec(memory_space=pltpu.VMEM)
    hbm = pl.BlockSpec(memory_space=pl.ANY)
    per_dev = K_COARSE * d // LANES
    dma = pltpu.SemaphoreType.DMA
    scratch = [pltpu.VMEM((3, blocks, cols, hi - lo), BF16) for lo, hi, _ in groups]
    scratch += [pltpu.VMEM((3, blocks - 1, cols, hi - lo), BF16) for lo, hi, _ in groups]
    scratch += [pltpu.VMEM((slots, d), BF16)]
    scratch += [pltpu.VMEM((r, fin), BF16) for r in rows]
    scratch += [pltpu.VMEM((4 * BORDER, d), BF16), pltpu.VMEM((blocks * per_dev, LANES), BF16)]
    scratch += [pltpu.VMEM((r, d), BF16) for r in rows]
    scratch += [pltpu.VMEM((r, d), F32) for r in rows]
    scratch += [pltpu.VMEM((r, d), F32) for r in rows]
    scratch += [pltpu.VMEM((r, 1), F32) for r in rows]
    scratch += [pltpu.VMEM((r, d), BF16) for r in rows]
    scratch += [pltpu.VMEM((r, d), BF16) for r in rows]
    scratch += [
        pltpu.VMEM(w_first.shape, BF16), pltpu.VMEM(w_second.shape, BF16),
        pltpu.VMEM((nodes, d), BF16), pltpu.VMEM((edges, d), BF16),
    ]
    scratch += [
        dma((5,)), dma((2, 9)), dma((2, 9)), dma((4,)), dma((4,)), dma((nlon,)), dma((nlon,)),
        dma((nlat,)), dma((nlat,)), dma((3, ngroups, steps)), dma((3, ngroups, steps)),
    ]
    updated_mesh, updated_edges, grads = pl.pallas_call(
        functools.partial(kernel, nlat, nlon, groups),
        out_shape=(
            jax.ShapeDtypeStruct((nodes, d), BF16),
            jax.ShapeDtypeStruct((edges, d), BF16),
            jax.ShapeDtypeStruct((3, cols, lanes), F32),
        ),
        in_specs=[
            vmem, vmem, vmem, vmem, vmem, hbm, vmem, vmem, hbm, vmem, hbm, vmem, hbm, hbm,
        ],
        out_specs=(vmem, vmem, vmem),
        scratch_shapes=scratch,
        compiler_params=pltpu.CompilerParams(
            collective_id=0, has_side_effects=True, vmem_limit_bytes=56 * 1024 * 1024
        ),
    )(
        grid_nodes, grid_edges, grid_sender.reshape(1, slots), owner_index.reshape(1, slots),
        mesh_nodes, mesh_edges, mesh_sender.reshape(1, edges), mesh_receiver.reshape(1, edges),
        w_first, first_bias, w_second, norm_gain, mesh_cotangent, edge_cotangent,
    )
    cut = fin // nlat
    grads = jnp.swapaxes(grads, 1, 2)
    return updated_mesh, updated_edges, grads[:, :cut], grads[:, cut:]


def solution(mesh):
    nlat, nlon = mesh.shape["lat"], mesh.shape["lon"]
    rows, flat = P(("lat", "lon"), None), P(("lat", "lon"))
    return jax.shard_map(
        functools.partial(shards, nlat, nlon),
        mesh=mesh,
        in_specs=(
            rows, rows, flat, flat, rows, rows, flat, flat, P(), P(), P(), P(), rows, rows,
        ),
        out_specs=(rows, rows, P(None, "lat", "lon"), P(None, "lat", "lon")),
        check_vma=False,
    )
```

```python
import functools

import jax
import jax.numpy as jnp
from jax import lax
from jax.experimental import pallas as pl
from jax.experimental.pallas import tpu as pltpu
from jax.sharding import PartitionSpec as P

BORDER = 64
K_COARSE = 4
EPSILON = 1e-05
LANES = 128
MESH = pl.DeviceIdType.MESH
F32 = jnp.float32
BF16 = jnp.bfloat16


def mm(a, b, ca=1, cb=0):
    return lax.dot_general(a, b, (((ca,), (cb,)), ((), ())), preferred_element_type=F32)


def onehot_t(index, count):
    rows = lax.broadcasted_iota(jnp.int32, (count, index.shape[1]), 0)
    return jnp.where(rows == index, 1.0, 0.0).astype(BF16)


def bits_of(count):
    return count.bit_length() - 1


def plan(nlat, nlon, lanes):
    lat = [("lat", b) for b in range(bits_of(nlat))]
    lon = [("lon", b) for b in range(bits_of(nlon))]
    core, rest = lon[:1], lon[1:]
    x_first = core + rest + lat
    y_first = core + rest[1:] + lat + rest[:1]
    z_first = core + lat + rest
    spare = (x_first, y_first, x_first)
    units = max(lanes // LANES, 1)
    cycle = (z_first, y_first, x_first)
    return [
        [spare[k] if u % 4 == 3 else cycle[u % 4] for u in range(units)] for k in range(3)
    ]


def kernel(nlat, nlon, orders, *refs):
    (gn_h, ge_h, gs, ow, mn_h, me_h, ms, mr, wf_h, fb, ws_h, ng, mc_h, ec_h) = refs[:14]
    (um_h, ue_h, gout) = refs[14:17]
    (
        grads, landed, um, ue, gn, mn,
        snd, x0, x1, x2, bord, coarse,
        h0, h1, h2, p0, p1, p2, n0, n1, n2, r0, r1, r2,
        pg0, pg1, pg2, og0, og1, og2,
        wf, ws, mc, ec,
        load_sem, slot_send, slot_recv, side_send, side_recv, row_send, row_recv, col_send, col_recv,
        red_send, red_recv,
    ) = refs[17:]
    units = len(orders[0])
    gs_row, ow_row = gs[...].reshape(1, gs.shape[0]), ow[...].reshape(1, ow.shape[0])
    ms_row, mr_row = ms[...].reshape(1, ms.shape[0]), mr[...].reshape(1, mr.shape[0])
    xs, hs, ps, ns, rs = (x0, x1, x2), (h0, h1, h2), (p0, p1, p2), (n0, n1, n2), (r0, r1, r2)
    pgs, ogs = (pg0, pg1, pg2), (og0, og1, og2)
    lat, lon = lax.axis_index("lat"), lax.axis_index("lon")
    nodes, d = mn.shape
    slots = ge_h.shape[0]
    cap = slots // 9
    edges = ue.shape[0]
    has = {-1: lat > 0, 1: lat < nlat - 1}

    def when(a, action):
        if a == 0:
            action()
        else:
            pl.when(has[a])(action)

    barrier = pltpu.get_barrier_semaphore()
    peers = [(lat, lax.rem(lon + s, nlon)) for s in range(1, nlon)]
    peers += [(lax.rem(lat + s, nlat), lon) for s in range(1, nlat)]
    peers += [
        (lax.rem(lat + a, nlat), lax.rem(lon + b, nlon))
        for a in (1, nlat - 1)
        for b in (1, nlon - 1)
    ]
    for peer in peers:
        pl.semaphore_signal(barrier, inc=1, device_id=peer, device_id_type=MESH)

    loads = [
        pltpu.make_async_copy(gn_h, gn, load_sem.at[0]),
        pltpu.make_async_copy(mn_h, mn, load_sem.at[1]),
        pltpu.make_async_copy(me_h, x1.at[:, pl.ds(0, d)], load_sem.at[2]),
        pltpu.make_async_copy(wf_h, wf, load_sem.at[3]),
        pltpu.make_async_copy(ws_h, ws, load_sem.at[4]),
        pltpu.make_async_copy(mc_h, mc, load_sem.at[5]),
        pltpu.make_async_copy(ec_h, ec, load_sem.at[6]),
        pltpu.make_async_copy(
            ge_h.at[pl.ds(4 * cap, cap)], x0.at[pl.ds(4 * cap, cap), pl.ds(0, d)], load_sem.at[7]
        ),
    ]
    for copy in loads:
        copy.start()

    loads[0].wait()
    snd[...] = mm(onehot_t(gs_row, gn.shape[0]), gn[...], 0, 0).astype(BF16)
    loads[1].wait()
    per_dev = K_COARSE * d // LANES
    tail = mn[nodes - 16 : nodes, :]
    out_row = lax.broadcasted_iota(jnp.int32, (per_dev, 16), 0)
    in_row = lax.broadcasted_iota(jnp.int32, (per_dev, 16), 1)
    staged = jnp.zeros((per_dev, LANES), F32)
    for q in range(d // LANES):
        pick = (out_row - q * K_COARSE == in_row - (16 - K_COARSE)) & (in_row >= 16 - K_COARSE)
        staged += mm(jnp.where(pick, 1.0, 0.0).astype(BF16), tail[:, q * LANES : (q + 1) * LANES])
    me_row = (lon * nlat + lat) * per_dev
    coarse[pl.ds(pl.multiple_of(me_row, 16), per_dev), :] = staged.astype(BF16)

    @pl.when(lat == 0)
    def _():
        x0[0 : 3 * cap, 0 : 2 * d] = jnp.zeros((3 * cap, 2 * d), BF16)
        bord[0:BORDER, :] = jnp.zeros((BORDER, d), BF16)

    @pl.when(lat == nlat - 1)
    def _():
        x0[6 * cap : 9 * cap, 0 : 2 * d] = jnp.zeros((3 * cap, 2 * d), BF16)
        bord[BORDER : 2 * BORDER, :] = jnp.zeros((BORDER, d), BF16)

    pl.semaphore_wait(barrier, len(peers))

    def slot_copy(o, part):
        a, b = o // 3 - 1, o % 3 - 1
        src = (ge_h, snd)[part]
        return pltpu.make_async_remote_copy(
            src_ref=src.at[pl.ds(o * cap, cap)],
            dst_ref=x0.at[pl.ds((8 - o) * cap, cap), pl.ds(part * d, d)],
            send_sem=slot_send.at[part, o],
            recv_sem=slot_recv.at[part, 8 - o],
            device_id=(lat + a, lax.rem(lon + b + nlon, nlon)),
            device_id_type=MESH,
        )

    def side_copy(side):
        a, b = ((1, 0), (-1, 0), (0, 1), (0, -1))[side]
        return pltpu.make_async_remote_copy(
            src_ref=mn.at[pl.ds(0, BORDER)],
            dst_ref=bord.at[pl.ds(side * BORDER, BORDER)],
            send_sem=side_send.at[side],
            recv_sem=side_recv.at[side],
            device_id=(lat + a, lax.rem(lon + b + nlon, nlon)),
            device_id_type=MESH,
        )

    side_a = (1, -1, 0, 0)
    def col_copy(s, incoming):
        other = lax.rem(lat - s + nlat, nlat) if incoming else lax.rem(lat + s, nlat)
        owner = other if incoming else lat
        span = pl.ds(pl.multiple_of((lon * nlat + owner) * per_dev, 16), per_dev)
        return pltpu.make_async_remote_copy(
            src_ref=coarse.at[span], dst_ref=coarse.at[span],
            send_sem=col_send.at[s], recv_sem=col_recv.at[s],
            device_id=(other, lon), device_id_type=MESH,
        )

    def row_copy(s, incoming):
        other = lax.rem(lon - s + nlon, nlon) if incoming else lax.rem(lon + s, nlon)
        owner = other if incoming else lon
        span = pl.ds(pl.multiple_of(owner * nlat * per_dev, 16), nlat * per_dev)
        return pltpu.make_async_remote_copy(
            src_ref=coarse.at[span], dst_ref=coarse.at[span],
            send_sem=row_send.at[s], recv_sem=row_recv.at[s],
            device_id=(lat, other), device_id_type=MESH,
        )

    remote_slots = [0, 2, 6, 8, 1, 7, 3, 5]
    for s in range(1, nlat):
        col_copy(s, False).start()
    for side in range(4):
        when(side_a[side], lambda side=side: side_copy(side).start())
    for part in (1, 0):
        for o in remote_slots:
            when(o // 3 - 1, lambda o=o, part=part: slot_copy(o, part).start())

    recv_t = onehot_t(mr_row, nodes)
    x1[:, 2 * d : 3 * d] = mm(recv_t, mn[...], 0, 0).astype(BF16)
    for s in range(1, nlat):
        col_copy(s, True).wait_recv()
    for s in range(1, nlon):
        row_copy(s, False).start()
    n1[...] = mm(onehot_t(ms_row, nodes), mn[...], 0, 0)
    x0[4 * cap : 5 * cap, d : 2 * d] = snd[4 * cap : 5 * cap, :]
    own_t = onehot_t(jnp.maximum(ow_row, 0), nodes)
    x0[:, 2 * d : 3 * d] = mm(own_t, mn[...], 0, 0).astype(BF16)
    x2[:, 0:d] = mn[...]
    loads[2].wait()
    loads[3].wait()
    p1[...] = (
        mm(x1[:, 0:d], wf[1, 0:d, :])
        + mm(x1[:, 2 * d : 3 * d], wf[1, 2 * d : 3 * d, :])
        + fb[1:2, :]
    )
    p0[...] = mm(x0[:, 2 * d : 3 * d], wf[0, 2 * d : 3 * d, :]) + fb[0:1, :]
    p2[...] = mm(mn[...], wf[2, 0:d, :]) + fb[2:3, :]
    loads[4].wait()
    late = ((0, 2 * d), (d, 2 * d), (d, 3 * d))

    def forward(k, lo, size):
        rows = pl.ds(lo, size)
        lo_in, hi_in = late[k]
        pre = ps[k][rows, :] + mm(xs[k][rows, lo_in:hi_in], wf[k, lo_in:hi_in, :])
        ps[k][rows, :] = pre
        hidden = (pre * jax.nn.sigmoid(pre)).astype(BF16)
        hs[k][rows, :] = hidden
        out = mm(hidden, ws[k])
        centred = out - jnp.mean(out, axis=-1, keepdims=True)
        scale = lax.rsqrt(jnp.mean(centred * centred, axis=-1, keepdims=True) + EPSILON)
        normed = centred * scale
        ns[k][rows, :] = normed
        rs[k][rows, :] = scale
        return normed * ng[k : k + 1, :]

    def backward(k, lo, size, dmsg):
        rows = pl.ds(lo, size)
        dn = dmsg * ng[k : k + 1, :]
        normed = ns[k][rows, :]
        dout = rs[k][rows, :] * (
            dn
            - jnp.mean(dn, axis=-1, keepdims=True)
            - normed * jnp.mean(dn * normed, axis=-1, keepdims=True)
        )
        og = dout.astype(BF16)
        ogs[k][rows, :] = og
        dh = mm(og, ws[k], 1, 1).astype(BF16).astype(F32)
        pre = ps[k][rows, :]
        gate = jax.nn.sigmoid(pre)
        pg = (dh * (gate * (1.0 + pre * (1.0 - gate)))).astype(BF16)
        pgs[k][rows, :] = pg
        return pg

    def tiles(count):
        size = 256 if count % 256 == 0 else count
        return [(i * size, size) for i in range(count // size)]

    for side in range(4):
        when(-side_a[side], lambda side=side: side_copy(side).wait_recv())
    n1[...] += mm(onehot_t(ms_row - nodes, 4 * BORDER), bord[...], 0, 0)
    for s in range(1, nlon):
        row_copy(s, True).wait_recv()
    rank = ms_row - (nodes + 4 * BORDER)
    owner = lax.shift_right_logical(rank, bits_of(K_COARSE))
    owner = (owner & (nlon - 1)) * nlat + lax.shift_right_logical(owner, bits_of(nlon))
    place = owner * per_dev + (rank & (K_COARSE - 1))
    for q in range(d // LANES):
        target = jnp.where(rank >= 0, place + q * K_COARSE, -1)
        picked = mm(onehot_t(target, coarse.shape[0]), coarse[...], 0, 0)
        span = slice(q * LANES, (q + 1) * LANES)
        x1[:, d + q * LANES : d + (q + 1) * LANES] = (n1[:, span] + picked).astype(BF16)
    total = 0.0
    for lo, size in tiles(edges):
        msg = forward(1, lo, size)
        ue[lo : lo + size, :] = (x1[lo : lo + size, 0:d].astype(F32) + msg).astype(BF16)
        total += mm(recv_t[:, lo : lo + size], msg.astype(BF16))
    x2[:, 2 * d : 3 * d] = total.astype(BF16)

    ue_out = pltpu.make_async_copy(ue, ue_h, load_sem.at[8])
    ue_out.start()

    loads[7].wait()
    for j in remote_slots:
        def arrive(j=j):
            slot_copy(8 - j, 0).wait_recv()
            slot_copy(8 - j, 1).wait_recv()
        when(j // 3 - 1, arrive)
    grid_msgs = [forward(0, lo, size).astype(BF16) for lo, size in tiles(slots)]
    grid_t = onehot_t(ow_row, nodes)
    total = 0.0
    for (lo, size), msg in zip(tiles(slots), grid_msgs):
        total += mm(grid_t[:, lo : lo + size], msg)
    x2[:, d : 2 * d] = total.astype(BF16)

    loads[5].wait()
    for lo, size in tiles(nodes):
        out = forward(2, lo, size)
        um[lo : lo + size, :] = (mn[lo : lo + size, :].astype(F32) + out).astype(BF16)
        backward(2, lo, size, mc[lo : lo + size, :].astype(F32))

    um_out = pltpu.make_async_copy(um, um_h, load_sem.at[9])
    um_out.start()

    blocks = nlat * nlon
    steps = bits_of(nlat) + bits_of(nlon)
    first_rows = x0.shape[1] // nlat
    second_rows = d // nlat
    block_cols = d // nlon
    unit = gout.shape[2] // units

    def place_of(order, l, c):
        at = 0
        for axis, bit in order:
            at = at * 2 + (((l if axis == "lat" else c) >> bit) & 1)
        return at

    def make_grads(k):
        width = 256
        for top in range(0, d, width):
            left = mm(pgs[k][:, top : top + width], xs[k][...], 0, 0).astype(BF16)
            right = mm(ogs[k][:, top : top + width], hs[k][...], 0, 0).astype(BF16)
            for u, order in enumerate(orders[k]):
                lo, hi = u * unit, (u + 1) * unit
                end, start = min(hi, first_rows), max(lo, first_rows)
                for l in range(nlat):
                    for i in range(width // block_cols):
                        at = place_of(order, l, top // block_cols + i)
                        cols = slice(i * block_cols, (i + 1) * block_cols)
                        if lo < end:
                            span = slice(l * first_rows + lo, l * first_rows + end)
                            grads[k, u, at, :, 0 : end - lo] = left[cols, span]
                        if start < hi:
                            from_row = l * second_rows - first_rows
                            span = slice(from_row + start, from_row + hi)
                            grads[k, u, at, :, start - lo : unit] = right[cols, span]

    def bit_at(order, i):
        axis, bit = order[i]
        return lax.rem((lat if axis == "lat" else lon) // (1 << bit), 2)

    def base_of(order, i):
        base = 0
        for step in range(i):
            base = base + bit_at(order, step) * (blocks >> (step + 1))
        return base

    def red_copy(k, u, i):
        order = orders[k][u]
        half = blocks >> (i + 1)
        axis, bit = order[i]
        mine = bit_at(order, i)
        shift = (1 - 2 * mine) * (1 << bit)
        peer = (lat + shift, lon) if axis == "lat" else (lat, lon + shift)
        return pltpu.make_async_remote_copy(
            src_ref=grads.at[k, u, pl.ds(base_of(order, i) + (1 - mine) * half, half)],
            dst_ref=landed.at[k, u, pl.ds(blocks - 2 * half, half)],
            send_sem=red_send.at[k, u, i],
            recv_sem=red_recv.at[k, u, i],
            device_id=peer,
            device_id_type=MESH,
        )

    def add(k, u, i, start, count):
        half = blocks >> (i + 1)
        base, from_block = base_of(orders[k][u], i + 1) + start, blocks - 2 * half + start

        def one(j, carry):
            grads[k, u, base + j] = grads[k, u, base + j] + landed[k, u, from_block + j]
            return carry

        lax.fori_loop(0, count, one, 0)

    def progress(k, i):
        for u in range(units):
            red_copy(k, u, i).wait_recv()
            if i + 1 < steps:
                quarter = blocks >> (i + 2)
                mine = bit_at(orders[k][u], i + 1)
                add(k, u, i, (1 - mine) * quarter, quarter)
                red_copy(k, u, i + 1).start()
                add(k, u, i, mine * quarter, quarter)
            else:
                gout[k, :, u * unit : (u + 1) * unit] = (
                    grads[k, u, base_of(orders[k][u], steps)].astype(F32)
                    + landed[k, u, blocks - 2].astype(F32)
                )

    def begin(k):
        make_grads(k)
        for u in range(units):
            red_copy(k, u, 0).start()

    begin(2)
    loads[6].wait()
    sums_cot = mm(pg2[...], wf[2, d : 3 * d, :], 1, 1).astype(BF16)
    for n, (lo, size) in enumerate(tiles(edges)):
        back = mm(recv_t[:, lo : lo + size], sums_cot[:, d : 2 * d], 0, 0)
        backward(1, lo, size, ec[lo : lo + size, :].astype(F32) + back)
        if n == 0:
            progress(2, 0)
    begin(1)
    for lo, size in tiles(slots):
        backward(0, lo, size, mm(grid_t[:, lo : lo + size], sums_cot[:, 0:d], 0, 0))
    progress(1, 0)
    begin(0)
    progress(2, 1)
    progress(0, 0)
    rest = [(i - k, -k, k, i) for k in range(3) for i in range(2 if k == 2 else 1, steps)]
    for _, _, k, i in sorted(rest):
        progress(k, i)

    ue_out.wait()
    um_out.wait()
    for o in remote_slots:
        def gone(o=o):
            slot_copy(o, 0).wait_send()
            slot_copy(o, 1).wait_send()
        when(o // 3 - 1, gone)
    for side in range(4):
        when(side_a[side], lambda side=side: side_copy(side).wait_send())
    for s in range(1, nlon):
        row_copy(s, False).wait_send()
    for s in range(1, nlat):
        col_copy(s, False).wait_send()
    for k in range(3):
        for u in range(units):
            for i in range(steps):
                red_copy(k, u, i).wait_send()


def hand_over(cut, um_in, ue_in, grads_in, um, ue, first, second, sems):
    copies = [
        pltpu.make_async_copy(um_in, um, sems.at[0]),
        pltpu.make_async_copy(ue_in, ue, sems.at[1]),
        pltpu.make_async_copy(grads_in.at[:, :, pl.ds(0, cut)], first, sems.at[2]),
        pltpu.make_async_copy(
            grads_in.at[:, :, pl.ds(cut, second.shape[2])], second, sems.at[3]
        ),
    ]
    for copy in copies:
        copy.start()
    for copy in copies:
        copy.wait()


def shards(
    nlat, nlon,
    grid_nodes, grid_edges, grid_sender, owner_index, mesh_nodes, mesh_edges, mesh_sender,
    mesh_receiver, w_first, first_bias, w_second, norm_gain, mesh_cotangent, edge_cotangent,
):
    d = grid_nodes.shape[1]
    slots, nodes, edges = grid_edges.shape[0], mesh_nodes.shape[0], mesh_edges.shape[0]
    fin = w_first.shape[1]
    blocks = nlat * nlon
    steps = bits_of(nlat) + bits_of(nlon)
    lanes = (fin + d) // nlat
    orders = plan(nlat, nlon, lanes)
    units = len(orders[0])
    cols = d // nlon
    rows = (slots, edges, nodes)
    vmem = pl.BlockSpec(memory_space=pltpu.VMEM)
    hbm = pl.BlockSpec(memory_space=pl.ANY)
    per_dev = K_COARSE * d // LANES
    dma = pltpu.SemaphoreType.DMA
    scratch = [
        pltpu.VMEM((3, units, blocks, cols, lanes // units), BF16),
        pltpu.VMEM((3, units, blocks - 1, cols, lanes // units), BF16),
        pltpu.VMEM((nodes, d), BF16), pltpu.VMEM((edges, d), BF16),
        pltpu.VMEM(grid_nodes.shape, BF16), pltpu.VMEM((nodes, d), BF16),
    ]
    scratch += [pltpu.VMEM((slots, d), BF16)]
    scratch += [pltpu.VMEM((r, fin), BF16) for r in rows]
    scratch += [pltpu.VMEM((4 * BORDER, d), BF16), pltpu.VMEM((blocks * per_dev, LANES), BF16)]
    scratch += [pltpu.VMEM((r, d), BF16) for r in rows]
    scratch += [pltpu.VMEM((r, d), F32) for r in rows]
    scratch += [pltpu.VMEM((r, d), F32) for r in rows]
    scratch += [pltpu.VMEM((r, 1), F32) for r in rows]
    scratch += [pltpu.VMEM((r, d), BF16) for r in rows]
    scratch += [pltpu.VMEM((r, d), BF16) for r in rows]
    scratch += [
        pltpu.VMEM(w_first.shape, BF16), pltpu.VMEM(w_second.shape, BF16),
        pltpu.VMEM((nodes, d), BF16), pltpu.VMEM((edges, d), BF16),
    ]
    scratch += [
        dma((10,)), dma((2, 9)), dma((2, 9)), dma((4,)), dma((4,)), dma((nlon,)), dma((nlon,)),
        dma((nlat,)), dma((nlat,)), dma((3, units, steps)), dma((3, units, steps)),
    ]
    updated_mesh, updated_edges, grads = pl.pallas_call(
        functools.partial(kernel, nlat, nlon, orders),
        out_shape=(
            jax.ShapeDtypeStruct((nodes, d), BF16),
            jax.ShapeDtypeStruct((edges, d), BF16),
            jax.ShapeDtypeStruct((3, cols, lanes), F32),
        ),
        in_specs=[
            hbm, hbm, vmem, vmem, hbm, hbm, vmem, vmem, hbm, vmem, hbm, vmem, hbm, hbm,
        ],
        out_specs=(hbm, hbm, vmem),
        scratch_shapes=scratch,
        compiler_params=pltpu.CompilerParams(
            collective_id=0, has_side_effects=True, vmem_limit_bytes=56 * 1024 * 1024
        ),
    )(
        grid_nodes, grid_edges, grid_sender, owner_index, mesh_nodes, mesh_edges,
        mesh_sender, mesh_receiver,
        w_first, first_bias, w_second, norm_gain, mesh_cotangent, edge_cotangent,
    )
    cut = fin // nlat
    if cut % LANES:
        grads = jnp.swapaxes(grads, 1, 2)
        return updated_mesh, updated_edges, grads[:, :cut], grads[:, cut:]
    updated_mesh, updated_edges, first, second = pl.pallas_call(
        functools.partial(hand_over, cut),
        out_shape=(
            jax.ShapeDtypeStruct((nodes, d), BF16),
            jax.ShapeDtypeStruct((edges, d), BF16),
            jax.ShapeDtypeStruct((3, cols, cut), F32),
            jax.ShapeDtypeStruct((3, cols, lanes - cut), F32),
        ),
        in_specs=[hbm, hbm, hbm],
        out_specs=(hbm, hbm, hbm, hbm),
        scratch_shapes=[dma((4,))],
    )(updated_mesh, updated_edges, grads)
    return updated_mesh, updated_edges, jnp.swapaxes(first, 1, 2), jnp.swapaxes(second, 1, 2)


def solution(mesh):
    nlat, nlon = mesh.shape["lat"], mesh.shape["lon"]
    rows, flat = P(("lat", "lon"), None), P(("lat", "lon"))
    return jax.shard_map(
        functools.partial(shards, nlat, nlon),
        mesh=mesh,
        in_specs=(
            rows, rows, flat, flat, rows, rows, flat, flat, P(), P(), P(), P(), rows, rows,
        ),
        out_specs=(rows, rows, P(None, "lat", "lon"), P(None, "lat", "lon")),
        check_vma=False,
    )
```

```python
import functools

import jax
import jax.numpy as jnp
from jax import lax
from jax.experimental import pallas as pl
from jax.experimental.pallas import tpu as pltpu
from jax.sharding import PartitionSpec as P

BORDER = 64
K_COARSE = 4
EPSILON = 1e-05
LANES = 128
MESH = pl.DeviceIdType.MESH
F32 = jnp.float32
BF16 = jnp.bfloat16


def mm(a, b, ca=1, cb=0):
    return lax.dot_general(a, b, (((ca,), (cb,)), ((), ())), preferred_element_type=F32)


def onehot_t(index, count):
    rows = lax.broadcasted_iota(jnp.int32, (count, index.shape[1]), 0)
    return jnp.where(rows == index, 1.0, 0.0).astype(BF16)


def bits_of(count):
    return count.bit_length() - 1


def plan(nlat, nlon, lanes):
    lat = [("lat", b) for b in range(bits_of(nlat))]
    lon = [("lon", b) for b in range(bits_of(nlon))]
    core, rest = lon[:1], lon[1:]
    x_first = core + rest + lat
    y_first = core + rest[1:] + lat + rest[:1]
    z_first = core + lat + rest
    spare = (x_first, y_first, x_first)
    units = max(lanes // LANES, 1)
    cycle = (z_first, y_first, x_first)
    return [
        [spare[k] if u % 4 == 3 else cycle[u % 4] for u in range(units)] for k in range(3)
    ]


def kernel(nlat, nlon, orders, *refs):
    (gn_h, ge_h, gs, ow, mn_h, me_h, ms, mr, wf_h, fb, ws_h, ng, mc_h, ec_h) = refs[:14]
    (um_h, ue_h, gout) = refs[14:17]
    (
        grads, landed, um, ue, gn, mn,
        snd, x0, x1, x2, bord, coarse,
        h0, h1, h2, p0, p1, p2, n0, n1, n2, r0, r1, r2,
        pg0, pg1, pg2, og0, og1, og2,
        wf, ws, mc, ec,
        load_sem, slot_send, slot_recv, side_send, side_recv, row_send, row_recv, col_send, col_recv,
        red_send, red_recv,
    ) = refs[17:]
    units = len(orders[0])
    blocks = nlat * nlon
    steps = bits_of(nlat) + bits_of(nlon)
    gs_row, ow_row = gs[...].reshape(1, gs.shape[0]), ow[...].reshape(1, ow.shape[0])
    ms_row, mr_row = ms[...].reshape(1, ms.shape[0]), mr[...].reshape(1, mr.shape[0])
    xs, hs, ps, ns, rs = (x0, x1, x2), (h0, h1, h2), (p0, p1, p2), (n0, n1, n2), (r0, r1, r2)
    pgs, ogs = (pg0, pg1, pg2), (og0, og1, og2)
    lat, lon = lax.axis_index("lat"), lax.axis_index("lon")
    nodes, d = mn.shape
    slots = ge_h.shape[0]
    cap = slots // 9
    edges = ue.shape[0]
    has = {-1: lat > 0, 1: lat < nlat - 1}

    def when(a, action):
        if a == 0:
            action()
        else:
            pl.when(has[a])(action)

    barrier = pltpu.get_barrier_semaphore()
    peers = [(lat, lax.rem(lon + s, nlon)) for s in range(1, nlon)]
    peers += [(lax.rem(lat + s, nlat), lon) for s in range(1, nlat)]
    peers += [
        (lax.rem(lat + a, nlat), lax.rem(lon + b, nlon))
        for a in (1, nlat - 1)
        for b in (1, nlon - 1)
    ]
    for peer in peers:
        pl.semaphore_signal(barrier, inc=1, device_id=peer, device_id_type=MESH)

    loads = [
        pltpu.make_async_copy(gn_h, gn, load_sem.at[0]),
        pltpu.make_async_copy(mn_h, mn, load_sem.at[1]),
        pltpu.make_async_copy(me_h, x1.at[:, pl.ds(0, d)], load_sem.at[2]),
        pltpu.make_async_copy(wf_h, wf, load_sem.at[3]),
        pltpu.make_async_copy(ws_h, ws, load_sem.at[4]),
        pltpu.make_async_copy(mc_h, mc, load_sem.at[5]),
        pltpu.make_async_copy(ec_h, ec, load_sem.at[6]),
        pltpu.make_async_copy(
            ge_h.at[pl.ds(4 * cap, cap)], x0.at[pl.ds(4 * cap, cap), pl.ds(0, d)], load_sem.at[7]
        ),
    ]
    for copy in loads:
        copy.start()

    loads[1].wait()
    per_dev = K_COARSE * d // LANES
    tail = mn[nodes - 16 : nodes, :]
    out_row = lax.broadcasted_iota(jnp.int32, (per_dev, 16), 0)
    in_row = lax.broadcasted_iota(jnp.int32, (per_dev, 16), 1)
    staged = jnp.zeros((per_dev, LANES), F32)
    for q in range(d // LANES):
        pick = (out_row - q * K_COARSE == in_row - (16 - K_COARSE)) & (in_row >= 16 - K_COARSE)
        staged += mm(jnp.where(pick, 1.0, 0.0).astype(BF16), tail[:, q * LANES : (q + 1) * LANES])
    me_row = (lon * nlat + lat) * per_dev
    coarse[pl.ds(pl.multiple_of(me_row, 16), per_dev), :] = staged.astype(BF16)

    @pl.when(lat == 0)
    def _():
        x0[0 : 3 * cap, 0 : 2 * d] = jnp.zeros((3 * cap, 2 * d), BF16)
        bord[0:BORDER, :] = jnp.zeros((BORDER, d), BF16)

    @pl.when(lat == nlat - 1)
    def _():
        x0[6 * cap : 9 * cap, 0 : 2 * d] = jnp.zeros((3 * cap, 2 * d), BF16)
        bord[BORDER : 2 * BORDER, :] = jnp.zeros((BORDER, d), BF16)

    pl.semaphore_wait(barrier, len(peers))

    def slot_copy(o, part):
        a, b = o // 3 - 1, o % 3 - 1
        src = (ge_h, snd)[part]
        return pltpu.make_async_remote_copy(
            src_ref=src.at[pl.ds(o * cap, cap)],
            dst_ref=x0.at[pl.ds((8 - o) * cap, cap), pl.ds(part * d, d)],
            send_sem=slot_send.at[part, o],
            recv_sem=slot_recv.at[part, 8 - o],
            device_id=(lat + a, lax.rem(lon + b + nlon, nlon)),
            device_id_type=MESH,
        )

    def side_copy(side):
        a, b = ((1, 0), (-1, 0), (0, 1), (0, -1))[side]
        return pltpu.make_async_remote_copy(
            src_ref=mn.at[pl.ds(0, BORDER)],
            dst_ref=bord.at[pl.ds(side * BORDER, BORDER)],
            send_sem=side_send.at[side],
            recv_sem=side_recv.at[side],
            device_id=(lat + a, lax.rem(lon + b + nlon, nlon)),
            device_id_type=MESH,
        )

    side_a = (1, -1, 0, 0)
    def col_copy(s, incoming):
        other = lax.rem(lat - s + nlat, nlat) if incoming else lax.rem(lat + s, nlat)
        owner = other if incoming else lat
        span = pl.ds(pl.multiple_of((lon * nlat + owner) * per_dev, 16), per_dev)
        return pltpu.make_async_remote_copy(
            src_ref=coarse.at[span], dst_ref=coarse.at[span],
            send_sem=col_send.at[s], recv_sem=col_recv.at[s],
            device_id=(other, lon), device_id_type=MESH,
        )

    def row_copy(s, incoming):
        other = lax.rem(lon - s + nlon, nlon) if incoming else lax.rem(lon + s, nlon)
        owner = other if incoming else lon
        span = pl.ds(pl.multiple_of(owner * nlat * per_dev, 16), nlat * per_dev)
        return pltpu.make_async_remote_copy(
            src_ref=coarse.at[span], dst_ref=coarse.at[span],
            send_sem=row_send.at[s], recv_sem=row_recv.at[s],
            device_id=(lat, other), device_id_type=MESH,
        )

    remote_slots = [0, 2, 6, 8, 1, 7, 3, 5]
    for s in range(1, nlat):
        col_copy(s, False).start()
    for side in range(4):
        when(side_a[side], lambda side=side: side_copy(side).start())
    for o in remote_slots:
        when(o // 3 - 1, lambda o=o: slot_copy(o, 0).start())
    loads[0].wait()
    snd[...] = mm(onehot_t(gs_row, gn.shape[0]), gn[...], 0, 0).astype(BF16)
    for o in remote_slots:
        when(o // 3 - 1, lambda o=o: slot_copy(o, 1).start())

    recv_t = onehot_t(mr_row, nodes)
    x1[:, 2 * d : 3 * d] = mm(recv_t, mn[...], 0, 0).astype(BF16)
    for s in range(1, nlat):
        col_copy(s, True).wait_recv()
    for s in range(1, nlon):
        row_copy(s, False).start()
    n1[...] = mm(onehot_t(ms_row, nodes), mn[...], 0, 0)
    x0[4 * cap : 5 * cap, d : 2 * d] = snd[4 * cap : 5 * cap, :]
    own_t = onehot_t(jnp.maximum(ow_row, 0), nodes)
    x0[:, 2 * d : 3 * d] = mm(own_t, mn[...], 0, 0).astype(BF16)
    x2[:, 0:d] = mn[...]
    loads[2].wait()
    loads[3].wait()
    p1[...] = (
        mm(x1[:, 0:d], wf[1, 0:d, :])
        + mm(x1[:, 2 * d : 3 * d], wf[1, 2 * d : 3 * d, :])
        + fb[1:2, :]
    )
    p0[...] = mm(x0[:, 2 * d : 3 * d], wf[0, 2 * d : 3 * d, :]) + fb[0:1, :]
    p2[...] = mm(mn[...], wf[2, 0:d, :]) + fb[2:3, :]
    loads[4].wait()
    late = ((0, 2 * d), (d, 2 * d), (d, 3 * d))

    def forward(k, lo, size):
        rows = pl.ds(lo, size)
        lo_in, hi_in = late[k]
        pre = ps[k][rows, :] + mm(xs[k][rows, lo_in:hi_in], wf[k, lo_in:hi_in, :])
        ps[k][rows, :] = pre
        hidden = (pre * jax.nn.sigmoid(pre)).astype(BF16)
        hs[k][rows, :] = hidden
        out = mm(hidden, ws[k])
        centred = out - jnp.mean(out, axis=-1, keepdims=True)
        scale = lax.rsqrt(jnp.mean(centred * centred, axis=-1, keepdims=True) + EPSILON)
        normed = centred * scale
        ns[k][rows, :] = normed
        rs[k][rows, :] = scale
        return normed * ng[k : k + 1, :]

    def backward(k, lo, size, dmsg):
        rows = pl.ds(lo, size)
        dn = dmsg * ng[k : k + 1, :]
        normed = ns[k][rows, :]
        dout = rs[k][rows, :] * (
            dn
            - jnp.mean(dn, axis=-1, keepdims=True)
            - normed * jnp.mean(dn * normed, axis=-1, keepdims=True)
        )
        og = dout.astype(BF16)
        ogs[k][rows, :] = og
        dh = mm(og, ws[k], 1, 1).astype(BF16).astype(F32)
        pre = ps[k][rows, :]
        gate = jax.nn.sigmoid(pre)
        pg = (dh * (gate * (1.0 + pre * (1.0 - gate)))).astype(BF16)
        pgs[k][rows, :] = pg
        return pg

    def tiles(count):
        size = 256 if count % 256 == 0 else count
        return [(i * size, size) for i in range(count // size)]

    for side in range(4):
        when(-side_a[side], lambda side=side: side_copy(side).wait_recv())
    for s in range(1, nlon):
        row_copy(s, True).wait_recv()
    shape = (blocks * K_COARSE, blocks * per_dev)
    entry = lax.broadcasted_iota(jnp.int32, shape, 0)
    packed = lax.broadcasted_iota(jnp.int32, shape, 1)
    owner = lax.shift_right_logical(entry, bits_of(K_COARSE))
    owner = (owner & (nlon - 1)) * nlat + lax.shift_right_logical(owner, bits_of(nlon))
    offset = packed - owner * per_dev - (entry & (K_COARSE - 1))
    for q in range(d // LANES):
        pick = jnp.where(offset == q * K_COARSE, 1.0, 0.0).astype(BF16)
        bord[4 * BORDER :, q * LANES : (q + 1) * LANES] = mm(pick, coarse[...]).astype(BF16)
    away = mm(onehot_t(ms_row - nodes, bord.shape[0]), bord[...], 0, 0)
    x1[:, d : 2 * d] = (n1[...] + away).astype(BF16)
    total = 0.0
    for lo, size in tiles(edges):
        msg = forward(1, lo, size)
        ue[lo : lo + size, :] = (x1[lo : lo + size, 0:d].astype(F32) + msg).astype(BF16)
        total += mm(recv_t[:, lo : lo + size], msg.astype(BF16))
    x2[:, 2 * d : 3 * d] = total.astype(BF16)

    ue_out = pltpu.make_async_copy(ue, ue_h, load_sem.at[8])
    ue_out.start()

    loads[7].wait()
    for j in remote_slots:
        def arrive(j=j):
            slot_copy(8 - j, 0).wait_recv()
            slot_copy(8 - j, 1).wait_recv()
        when(j // 3 - 1, arrive)
    grid_msgs = [forward(0, lo, size).astype(BF16) for lo, size in tiles(slots)]
    grid_t = onehot_t(ow_row, nodes)
    total = 0.0
    for (lo, size), msg in zip(tiles(slots), grid_msgs):
        total += mm(grid_t[:, lo : lo + size], msg)
    x2[:, d : 2 * d] = total.astype(BF16)

    loads[5].wait()
    for lo, size in tiles(nodes):
        out = forward(2, lo, size)
        um[lo : lo + size, :] = (mn[lo : lo + size, :].astype(F32) + out).astype(BF16)
        backward(2, lo, size, mc[lo : lo + size, :].astype(F32))

    um_out = pltpu.make_async_copy(um, um_h, load_sem.at[9])
    um_out.start()

    first_rows = x0.shape[1] // nlat
    second_rows = d // nlat
    block_cols = d // nlon
    unit = gout.shape[2] // units

    def place_of(order, l, c):
        at = 0
        for axis, bit in order:
            at = at * 2 + (((l if axis == "lat" else c) >> bit) & 1)
        return at

    def make_grads(k):
        width = 256
        for top in range(0, d, width):
            left = mm(pgs[k][:, top : top + width], xs[k][...], 0, 0).astype(BF16)
            right = mm(ogs[k][:, top : top + width], hs[k][...], 0, 0).astype(BF16)
            for u, order in enumerate(orders[k]):
                lo, hi = u * unit, (u + 1) * unit
                end, start = min(hi, first_rows), max(lo, first_rows)
                for l in range(nlat):
                    for i in range(width // block_cols):
                        at = place_of(order, l, top // block_cols + i)
                        cols = slice(i * block_cols, (i + 1) * block_cols)
                        if lo < end:
                            span = slice(l * first_rows + lo, l * first_rows + end)
                            grads[k, u, at, :, 0 : end - lo] = left[cols, span]
                        if start < hi:
                            from_row = l * second_rows - first_rows
                            span = slice(from_row + start, from_row + hi)
                            grads[k, u, at, :, start - lo : unit] = right[cols, span]

    def bit_at(order, i):
        axis, bit = order[i]
        return lax.rem((lat if axis == "lat" else lon) // (1 << bit), 2)

    def base_of(order, i):
        base = 0
        for step in range(i):
            base = base + bit_at(order, step) * (blocks >> (step + 1))
        return base

    def red_copy(k, u, i):
        order = orders[k][u]
        half = blocks >> (i + 1)
        axis, bit = order[i]
        mine = bit_at(order, i)
        shift = (1 - 2 * mine) * (1 << bit)
        peer = (lat + shift, lon) if axis == "lat" else (lat, lon + shift)
        return pltpu.make_async_remote_copy(
            src_ref=grads.at[k, u, pl.ds(base_of(order, i) + (1 - mine) * half, half)],
            dst_ref=landed.at[k, u, pl.ds(blocks - 2 * half, half)],
            send_sem=red_send.at[k, u, i],
            recv_sem=red_recv.at[k, u, i],
            device_id=peer,
            device_id_type=MESH,
        )

    def add(k, u, i, start, count):
        half = blocks >> (i + 1)
        base, from_block = base_of(orders[k][u], i + 1) + start, blocks - 2 * half + start

        step = min(count, 8)
        for j in range(0, count, step):
            to, frm = pl.ds(base + j, step), pl.ds(from_block + j, step)
            grads[k, u, to] = grads[k, u, to] + landed[k, u, frm]

    def progress(k, i):
        for u in range(units):
            red_copy(k, u, i).wait_recv()
            if i + 1 < steps:
                quarter = blocks >> (i + 2)
                mine = bit_at(orders[k][u], i + 1)
                add(k, u, i, (1 - mine) * quarter, quarter)
                red_copy(k, u, i + 1).start()
                add(k, u, i, mine * quarter, quarter)
            else:
                gout[k, :, u * unit : (u + 1) * unit] = (
                    grads[k, u, base_of(orders[k][u], steps)].astype(F32)
                    + landed[k, u, blocks - 2].astype(F32)
                )

    def begin(k):
        make_grads(k)
        for u in range(units):
            red_copy(k, u, 0).start()

    begin(2)
    loads[6].wait()
    sums_cot = mm(pg2[...], wf[2, d : 3 * d, :], 1, 1).astype(BF16)
    for n, (lo, size) in enumerate(tiles(edges)):
        back = mm(recv_t[:, lo : lo + size], sums_cot[:, d : 2 * d], 0, 0)
        backward(1, lo, size, ec[lo : lo + size, :].astype(F32) + back)
        if n == 0:
            progress(2, 0)
    begin(1)
    for lo, size in tiles(slots):
        backward(0, lo, size, mm(grid_t[:, lo : lo + size], sums_cot[:, 0:d], 0, 0))
    progress(1, 0)
    begin(0)
    progress(2, 1)
    progress(0, 0)
    rest = [(i - k, -k, k, i) for k in range(3) for i in range(2 if k == 2 else 1, steps)]
    for _, _, k, i in sorted(rest):
        progress(k, i)

    ue_out.wait()
    um_out.wait()
    for o in remote_slots:
        def gone(o=o):
            slot_copy(o, 0).wait_send()
            slot_copy(o, 1).wait_send()
        when(o // 3 - 1, gone)
    for side in range(4):
        when(side_a[side], lambda side=side: side_copy(side).wait_send())
    for s in range(1, nlon):
        row_copy(s, False).wait_send()
    for s in range(1, nlat):
        col_copy(s, False).wait_send()
    for k in range(3):
        for u in range(units):
            for i in range(steps):
                red_copy(k, u, i).wait_send()


def hand_over(cut, um_in, ue_in, grads_in, um, ue, first, second):
    um[...] = um_in[...]
    ue[...] = ue_in[...]
    first[...] = grads_in[:, :, 0:cut]
    second[...] = grads_in[:, :, cut:]


def shards(
    nlat, nlon,
    grid_nodes, grid_edges, grid_sender, owner_index, mesh_nodes, mesh_edges, mesh_sender,
    mesh_receiver, w_first, first_bias, w_second, norm_gain, mesh_cotangent, edge_cotangent,
):
    d = grid_nodes.shape[1]
    slots, nodes, edges = grid_edges.shape[0], mesh_nodes.shape[0], mesh_edges.shape[0]
    fin = w_first.shape[1]
    blocks = nlat * nlon
    steps = bits_of(nlat) + bits_of(nlon)
    lanes = (fin + d) // nlat
    orders = plan(nlat, nlon, lanes)
    units = len(orders[0])
    cols = d // nlon
    rows = (slots, edges, nodes)
    vmem = pl.BlockSpec(memory_space=pltpu.VMEM)
    hbm = pl.BlockSpec(memory_space=pl.ANY)
    per_dev = K_COARSE * d // LANES
    dma = pltpu.SemaphoreType.DMA
    scratch = [
        pltpu.VMEM((3, units, blocks, cols, lanes // units), BF16),
        pltpu.VMEM((3, units, blocks - 1, cols, lanes // units), BF16),
        pltpu.VMEM((nodes, d), BF16), pltpu.VMEM((edges, d), BF16),
        pltpu.VMEM(grid_nodes.shape, BF16), pltpu.VMEM((nodes, d), BF16),
    ]
    scratch += [pltpu.VMEM((slots, d), BF16)]
    scratch += [pltpu.VMEM((r, fin), BF16) for r in rows]
    scratch += [pltpu.VMEM((4 * BORDER + blocks * K_COARSE, d), BF16), pltpu.VMEM((blocks * per_dev, LANES), BF16)]
    scratch += [pltpu.VMEM((r, d), BF16) for r in rows]
    scratch += [pltpu.VMEM((r, d), F32) for r in rows]
    scratch += [pltpu.VMEM((r, d), F32) for r in rows]
    scratch += [pltpu.VMEM((r, 1), F32) for r in rows]
    scratch += [pltpu.VMEM((r, d), BF16) for r in rows]
    scratch += [pltpu.VMEM((r, d), BF16) for r in rows]
    scratch += [
        pltpu.VMEM(w_first.shape, BF16), pltpu.VMEM(w_second.shape, BF16),
        pltpu.VMEM((nodes, d), BF16), pltpu.VMEM((edges, d), BF16),
    ]
    scratch += [
        dma((10,)), dma((2, 9)), dma((2, 9)), dma((4,)), dma((4,)), dma((nlon,)), dma((nlon,)),
        dma((nlat,)), dma((nlat,)), dma((3, units, steps)), dma((3, units, steps)),
    ]
    updated_mesh, updated_edges, grads = pl.pallas_call(
        functools.partial(kernel, nlat, nlon, orders),
        out_shape=(
            jax.ShapeDtypeStruct((nodes, d), BF16),
            jax.ShapeDtypeStruct((edges, d), BF16),
            jax.ShapeDtypeStruct((3, cols, lanes), F32),
        ),
        in_specs=[
            hbm, hbm, vmem, vmem, hbm, hbm, vmem, vmem, hbm, vmem, hbm, vmem, hbm, hbm,
        ],
        out_specs=(hbm, hbm, vmem),
        scratch_shapes=scratch,
        compiler_params=pltpu.CompilerParams(
            collective_id=0, has_side_effects=True, vmem_limit_bytes=56 * 1024 * 1024
        ),
    )(
        grid_nodes, grid_edges, grid_sender, owner_index, mesh_nodes, mesh_edges,
        mesh_sender, mesh_receiver,
        w_first, first_bias, w_second, norm_gain, mesh_cotangent, edge_cotangent,
    )
    cut = fin // nlat
    if cut % LANES:
        grads = jnp.swapaxes(grads, 1, 2)
        return updated_mesh, updated_edges, grads[:, :cut], grads[:, cut:]
    updated_mesh, updated_edges, first, second = pl.pallas_call(
        functools.partial(hand_over, cut),
        out_shape=(
            jax.ShapeDtypeStruct((nodes, d), BF16),
            jax.ShapeDtypeStruct((edges, d), BF16),
            jax.ShapeDtypeStruct((3, cols, cut), F32),
            jax.ShapeDtypeStruct((3, cols, lanes - cut), F32),
        ),
        in_specs=[vmem, vmem, vmem],
        out_specs=(vmem, vmem, vmem, vmem),
    )(updated_mesh, updated_edges, grads)
    return updated_mesh, updated_edges, jnp.swapaxes(first, 1, 2), jnp.swapaxes(second, 1, 2)


def solution(mesh):
    nlat, nlon = mesh.shape["lat"], mesh.shape["lon"]
    rows, flat = P(("lat", "lon"), None), P(("lat", "lon"))
    return jax.shard_map(
        functools.partial(shards, nlat, nlon),
        mesh=mesh,
        in_specs=(
            rows, rows, flat, flat, rows, rows, flat, flat, P(), P(), P(), P(), rows, rows,
        ),
        out_specs=(rows, rows, P(None, "lat", "lon"), P(None, "lat", "lon")),
        check_vma=False,
    )
```
